256 devices in a mesh: ctx: 64 (over y, x, z_hi, core), tp: 4 (over z_lo).
Axes of the slice: x: 4, y: 4, z: 8 (z_hi: 2, z_lo: 4; z = z_hi * 4 + z_lo), core: 2. Of those that a mesh axis runs over, the one named last changes fastest.
Arguments:
- q_field: bfloat16 [4096, 16384], P('tp', 'ctx'), may hold values from -6 to 6
- k_field: bfloat16 [4096, 16384], P('tp', 'ctx'), may hold values from -6 to 6
- v_field: bfloat16 [4096, 16384], P('tp', 'ctx'), may hold values from -6 to 6
- out_grad: bfloat16 [4096, 16384], P('tp', 'ctx'), may hold values from -6 to 6
- filter_taps: float32 [4096, 16384], P('tp', 'ctx'), may hold values from -6 to 6
- skip: float32 [4096], P('tp'), may hold values from 0.5 to 1.5
Outputs:
- q_grad: bfloat16 [4096, 16384], P('tp', 'ctx')
- k_grad: bfloat16 [4096, 16384], P('tp', 'ctx')
- v_grad: bfloat16 [4096, 16384], P('tp', 'ctx')
- filter_grad: float32 [4096, 16384], P('tp', 'ctx')
The draws below stay inside these ranges and needn't reach their ends.
All inputs are finite; a program needn't handle non-finite values.
Results may differ from the reference program's by a relative error of at most 0.012.
Values may be sent and summed in bfloat16 or wider, within the bound.
A program may use at most 128 MiB of HBM per device.

```python
import jax
import jax.numpy as jnp
from jax import lax

CHANNEL_COUNT = 4096
TOKEN_TOTAL = 16384


def draw_filter_taps(key, part):
    key = jax.random.fold_in(key, 7)
    keys = jax.random.split(key, 6)
    slow_share = 0.5
    lag_grid = jnp.arange(TOKEN_TOTAL).astype(jnp.float32)
    slow = jax.random.uniform(keys[0], (CHANNEL_COUNT,)) < slow_share
    slow_rate = jnp.exp(jax.random.uniform(keys[1], (CHANNEL_COUNT,), minval=jnp.log(0.1), maxval=jnp.log(2.0))) / TOKEN_TOTAL
    fast_rate = jnp.exp(jax.random.uniform(keys[2], (CHANNEL_COUNT,), minval=jnp.log(2.0 / TOKEN_TOTAL), maxval=jnp.log(1.0 / 30.0)))
    fading_speed = jnp.where(slow, slow_rate, fast_rate)
    places = jax.random.randint(keys[3], (CHANNEL_COUNT, 3), 0, TOKEN_TOTAL)
    shrink_multipliers = jax.random.uniform(keys[4], (CHANNEL_COUNT, 3), minval=0.5, maxval=0.8)
    fading_pulse = jnp.ones((CHANNEL_COUNT, TOKEN_TOTAL), jnp.float32)
    for token_offset in range(3):
        trailing_remainder = lag_grid[None, :] >= places[:, token_offset][:, None].astype(jnp.float32)
        fading_pulse = fading_pulse * jnp.where(trailing_remainder, shrink_multipliers[:, token_offset][:, None], 1.0)
    fading_profile = jnp.exp(-fading_speed[:, None] * lag_grid[None, :]) * fading_pulse
    total = jnp.expm1(-2.0 * fading_speed * TOKEN_TOTAL) / jnp.expm1(-2.0 * fading_speed)
    noise = jax.random.truncated_normal(keys[5], -6.0, 6.0, (CHANNEL_COUNT, TOKEN_TOTAL))
    return (noise * fading_profile / jnp.sqrt(total)[:, None]).astype(jnp.float32)


def block_levels(rng, dims, shards, low, high):
    def one(dim, shards_of):
        heights = jax.random.uniform(jax.random.fold_in(jax.random.fold_in(rng, 6), dim), (shards_of,), jnp.float32, low / len(shards), high / len(shards))
        return jnp.repeat(jnp.exp(heights), dims[dim] // shards_of).reshape((-1,) + (1,) * (len(dims) - dim - 1))

    level = one(*shards[0])
    for cut in shards[1:]:
        level = level * one(*cut)
    return level


def normal_values(key, dims, scale, bound, cuts=(), held_as=jnp.bfloat16):
    entries = jax.random.normal(key, dims, jnp.float32) * scale
    if len(cuts) > 0:
        entries = block_levels(key, dims, cuts, -0.22, 0.18) * entries
    return jnp.clip(entries, min=-bound, max=bound).astype(held_as)


def setup_inputs(seed: int = 0) -> dict:
    key_of = jax.random.split(jax.random.key(seed), 7)
    return {
        "q_field": normal_values(key_of[0], (CHANNEL_COUNT, TOKEN_TOTAL), 1.0, 6.0, ((0, 4), (1, 64))),
        "k_field": normal_values(key_of[1], (CHANNEL_COUNT, TOKEN_TOTAL), 1.0, 6.0, ((0, 4), (1, 64))),
        "v_field": normal_values(key_of[2], (CHANNEL_COUNT, TOKEN_TOTAL), 1.0, 6.0, ((0, 4), (1, 64))),
        "out_grad": normal_values(key_of[3], (CHANNEL_COUNT, TOKEN_TOTAL), 1.0, 6.0, ((0, 4), (1, 64))),
        "filter_taps": draw_filter_taps(jax.random.fold_in(key_of[6], 71), 0),
        "skip": jnp.clip(0.5 + 1.0 * jax.random.uniform(key_of[5], (CHANNEL_COUNT,), jnp.float32) ** block_levels(key_of[5], (CHANNEL_COUNT,), ((0, 4),), -0.2, 0.2), 0.5, 1.5),
    }


def block_convolve(pieces):
    gated_block, product_block, taps_block = pieces
    length = gated_block.shape[-1]
    n_len = 2 * length
    gated_spec = jnp.fft.rfft(gated_block, n=n_len, axis=-1)
    product_spec = jnp.fft.rfft(product_block, n=n_len, axis=-1)
    taps_spec = jnp.fft.rfft(taps_block, n=n_len, axis=-1)
    forward = jnp.fft.irfft(gated_spec * taps_spec, n=n_len, axis=-1)[:, :length]
    backward = jnp.fft.irfft(product_spec * jnp.conj(taps_spec), n=n_len, axis=-1)[:, :length]
    taps_grad = jnp.fft.irfft(product_spec * jnp.conj(gated_spec), n=n_len, axis=-1)[:, :length]
    return forward, backward, taps_grad * (length ** -0.5)


def reference(q_field, k_field, v_field, out_grad, filter_taps, skip):
    gated = (k_field.astype(jnp.float32) * v_field.astype(jnp.float32)).astype(jnp.bfloat16)
    product = (out_grad.astype(jnp.float32) * q_field.astype(jnp.float32)).astype(jnp.bfloat16)
    length = gated.shape[1]
    block = 64
    gated_blocks = gated.astype(jnp.float32).reshape(CHANNEL_COUNT // block, block, length)
    product_blocks = product.astype(jnp.float32).reshape(CHANNEL_COUNT // block, block, length)
    taps_blocks = filter_taps.reshape(CHANNEL_COUNT // block, block, length)
    forward, backward, taps_grad = lax.map(block_convolve, (gated_blocks, product_blocks, taps_blocks))
    forward = forward.reshape(CHANNEL_COUNT, length)
    backward = backward.reshape(CHANNEL_COUNT, length)
    taps_grad = taps_grad.reshape(CHANNEL_COUNT, length).astype(jnp.float32)
    forward_b = lax.optimization_barrier(forward.astype(jnp.bfloat16)).astype(jnp.float32)
    backward_b = lax.optimization_barrier(backward.astype(jnp.bfloat16)).astype(jnp.float32)
    skip_col = skip[:, None]
    q_grad = (out_grad.astype(jnp.float32) * (forward_b + skip_col * gated.astype(jnp.float32))).astype(jnp.bfloat16)
    z_grad = backward_b + skip_col * product.astype(jnp.float32)
    k_grad = (v_field.astype(jnp.float32) * z_grad).astype(jnp.bfloat16)
    v_grad = (k_field.astype(jnp.float32) * z_grad).astype(jnp.bfloat16)
    return q_grad, k_grad, v_grad, taps_grad
```

```python
import functools

import jax
import jax.numpy as jnp
import ml_dtypes
import numpy as np
from jax import lax
from jax.experimental import pallas as pl
from jax.experimental.pallas import tpu as pltpu
from jax.sharding import PartitionSpec as P

MESH = pl.DeviceIdType.MESH
BF16 = jnp.bfloat16
F32 = jnp.float32


def split_table(table, axis):
    high = table.astype(ml_dtypes.bfloat16)
    low = (table - high.astype(np.float64)).astype(ml_dtypes.bfloat16)
    return np.concatenate([high, low], axis=axis)


def make_tables(blocks, width):
    a = np.arange(blocks)[:, None]
    c = np.arange(blocks)[None, :] + 0.5
    phase = 2 * np.pi * a * c / (2 * blocks)
    first = split_table(np.concatenate([np.cos(phase).T, -np.sin(phase).T], axis=0), 1)
    last = split_table(np.concatenate([np.cos(phase), -np.sin(phase)], axis=1), 1)
    b = np.arange(width)
    turn = 2 * np.pi * c.T * b[None, :] / (2 * blocks * width)
    twist = np.concatenate([np.cos(turn), np.sin(turn)], axis=0).astype(np.float32)
    angle = 2 * np.pi * ((b[:, None] * b[None, :]) % width) / width
    cos, sin = np.cos(angle), np.sin(angle)
    forth = np.block([[cos, -sin], [sin, cos]]).astype(ml_dtypes.bfloat16)
    back = np.block([[cos, sin], [-sin, cos]]).astype(ml_dtypes.bfloat16)
    return first, last, twist, forth, back


def dot(x, y):
    return jnp.dot(x, y, preferred_element_type=F32)


def kernel(
    blocks, count, width,
    k_hbm, v_hbm, g_hbm, q_hbm, taps_hbm, first_hbm, last_hbm, twist_hbm, forth_hbm, back_hbm,
    fwd_out, bwd_out, tap_out,
    k_in, v_in, g_in, q_in, taps_in, first, last, twist, forth, back,
    sent, arrived, packed, wide, gated_spec, taps_spec, prod_spec, mixed,
    load_sem, own_sem, send_sem, recv_sem,
):
    me = lax.axis_index("ctx")
    rows = blocks * count
    lanes = 128
    halves = width // lanes
    loads = [
        pltpu.make_async_copy(src, dst, load_sem.at[i])
        for i, (src, dst) in enumerate(
            (
                (k_hbm, k_in), (v_hbm, v_in), (taps_hbm, taps_in), (g_hbm, g_in), (q_hbm, q_in),
                (first_hbm, first), (last_hbm, last), (twist_hbm, twist), (forth_hbm, forth), (back_hbm, back),
            )
        )
    ]
    for load in loads:
        load.start()

    barrier = pltpu.get_barrier_semaphore()

    def greet(j, carry):
        peer = lax.rem(me + j, blocks)
        pl.semaphore_signal(barrier, inc=1, device_id={"ctx": peer}, device_id_type=MESH)
        return carry

    lax.fori_loop(1, blocks, greet, 0)

    def own_rows():
        return pl.ds(pl.multiple_of(me * count, count), count)

    def send(i, target):
        def one(j, carry):
            peer = lax.rem(me + j, blocks)
            pltpu.make_async_remote_copy(
                src_ref=sent.at[i, pl.ds(pl.multiple_of(peer * count, count), count)],
                dst_ref=target.at[own_rows()],
                send_sem=send_sem.at[i],
                recv_sem=recv_sem.at[i],
                device_id={"ctx": peer},
                device_id_type=MESH,
            ).start()
            return carry

        lax.fori_loop(1, blocks, one, 0)

    def wait_all(i, target, sem):
        part = pl.ds(0, rows - count)
        pltpu.make_async_copy(target.at[part], target.at[part], sem.at[i]).wait()

    loads[0].wait()
    loads[1].wait()
    sent[0] = (k_in[...].astype(F32) * v_in[...].astype(F32)).astype(BF16)
    pl.semaphore_wait(barrier, blocks - 1)
    send(0, arrived.at[0])
    loads[2].wait()
    sent[1] = taps_in[...].astype(BF16)
    send(1, arrived.at[1])
    loads[3].wait()
    loads[4].wait()
    sent[2] = (g_in[...].astype(F32) * q_in[...].astype(F32)).astype(BF16)
    send(2, arrived.at[2])
    for load in loads[5:]:
        load.wait()

    group = 4
    tile = group * blocks

    def transform(i, spec):
        wait_all(i, arrived.at[i], recv_sem)
        arrived[i, own_rows()] = sent[i, own_rows()]
        for h in range(halves):
            wide[h] = arrived[i, :, lanes * h : lanes * (h + 1)].astype(F32)

        def one(t, carry):
            for s in range(group):
                every = pl.ds(t * group + s, blocks, stride=count)
                x = jnp.concatenate([wide[h, every, :] for h in range(halves)], axis=1).astype(BF16)
                y = dot(first[...], jnp.concatenate([x, x], axis=0))
                real, imag = y[:blocks], y[blocks:]
                cos, sin = twist[:blocks], twist[blocks:]
                packed[s * blocks : (s + 1) * blocks, :width] = (real * cos + imag * sin).astype(BF16)
                packed[s * blocks : (s + 1) * blocks, width:] = (imag * cos - real * sin).astype(BF16)
            spec[pl.ds(pl.multiple_of(t * tile, tile), tile), :] = dot(packed[...], forth[...])
            return carry

        lax.fori_loop(0, count // group, one, 0)

    def multiply_back(i, left, right, conjugate, scale):
        def one(t, carry):
            part = pl.ds(pl.multiple_of(t * tile, tile), tile)
            lr, li = left[part, :width], left[part, width:]
            rr, ri = right[part, :width], right[part, width:]
            if conjugate:
                mixed[:, :width] = (lr * rr + li * ri).astype(BF16)
                mixed[:, width:] = (li * rr - lr * ri).astype(BF16)
            else:
                mixed[:, :width] = (lr * rr - li * ri).astype(BF16)
                mixed[:, width:] = (lr * ri + li * rr).astype(BF16)
            u = dot(mixed[...], back[...])
            cos, sin = twist[:blocks] * scale, twist[blocks:] * scale
            for s in range(group):
                real = u[s * blocks : (s + 1) * blocks, :width]
                imag = u[s * blocks : (s + 1) * blocks, width:]
                turned = jnp.concatenate(
                    [(real * cos - imag * sin).astype(BF16), (imag * cos + real * sin).astype(BF16)], axis=0
                )
                out = dot(last[...], jnp.concatenate([turned, turned], axis=0))
                for h in range(halves):
                    wide[h, pl.ds(t * group + s, blocks, stride=count), :] = out[:, lanes * h : lanes * (h + 1)]
            return carry

        lax.fori_loop(0, count // group, one, 0)
        for h in range(halves):
            sent[i, :, lanes * h : lanes * (h + 1)] = wide[h].astype(BF16)

    def give(i, out):
        own = pltpu.make_async_copy(sent.at[i, own_rows()], out.at[own_rows()], own_sem.at[i - 3])
        send(i, out)
        own.start()
        return own

    norm = 1.0 / (blocks * width)
    transform(0, gated_spec)
    transform(1, taps_spec)
    multiply_back(3, gated_spec, taps_spec, False, norm)
    owns = [give(3, fwd_out)]
    transform(2, prod_spec)
    multiply_back(4, prod_spec, taps_spec, True, norm)
    owns.append(give(4, bwd_out))
    multiply_back(5, prod_spec, gated_spec, True, norm * (blocks * width) ** -0.5)
    owns.append(give(5, tap_out))
    for own in owns:
        own.wait()
    for i in range(6):
        wait_all(i, sent.at[i], send_sem)
    for i, out in ((3, fwd_out), (4, bwd_out), (5, tap_out)):
        wait_all(i, out, recv_sem)


def exchange_convolve(k_field, v_field, out_grad, q_field, taps, blocks):
    channels, width = k_field.shape
    count = channels // blocks
    rows = channels
    tables = make_tables(blocks, width)
    any_space = pl.BlockSpec(memory_space=pl.ANY)
    field = pltpu.VMEM((rows, width), BF16)
    spectrum = pltpu.VMEM((rows, 2 * width), F32)
    table_space = [pltpu.VMEM(t.shape, t.dtype) for t in tables]
    dma = pltpu.SemaphoreType.DMA
    return pl.pallas_call(
        functools.partial(kernel, blocks, count, width),
        out_shape=[jax.ShapeDtypeStruct((rows, width), BF16)] * 3,
        in_specs=[any_space] * 10,
        out_specs=[any_space] * 3,
        scratch_shapes=[
            field, field, field, field, pltpu.VMEM((rows, width), F32), *table_space,
            pltpu.VMEM((6, rows, width), BF16),
            pltpu.VMEM((3, rows, width), BF16),
            pltpu.VMEM((4 * blocks, 2 * width), BF16),
            pltpu.VMEM((width // 128, rows, 128), F32),
            spectrum, spectrum, spectrum,
            pltpu.VMEM((4 * blocks, 2 * width), BF16),
            dma((10,)), dma((3,)), dma((6,)), dma((6,)),
        ],
        compiler_params=pltpu.CompilerParams(
            collective_id=0, has_side_effects=True, vmem_limit_bytes=48 * 2**20
        ),
        name="exchange_convolve",
    )(k_field, v_field, out_grad, q_field, taps, *[jnp.asarray(t) for t in tables])


def local(blocks, q_field, k_field, v_field, out_grad, filter_taps, skip):
    fwd, bwd, tap = exchange_convolve(k_field, v_field, out_grad, q_field, filter_taps, blocks)
    wide = lambda x: x.astype(F32)
    skip_col = skip[:, None]
    gated = wide((wide(k_field) * wide(v_field)).astype(BF16))
    product = wide((wide(out_grad) * wide(q_field)).astype(BF16))
    q_grad = (wide(out_grad) * (wide(fwd) + skip_col * gated)).astype(BF16)
    z_grad = wide(bwd) + skip_col * product
    k_grad = (wide(v_field) * z_grad).astype(BF16)
    v_grad = (wide(k_field) * z_grad).astype(BF16)
    return q_grad, k_grad, v_grad, wide(tap)


def solution(mesh):
    spec = P("tp", "ctx")
    return jax.shard_map(
        functools.partial(local, mesh.shape["ctx"]),
        mesh=mesh,
        in_specs=(spec, spec, spec, spec, spec, P("tp")),
        out_specs=(spec, spec, spec, spec),
        check_vma=False,
    )
```

```python
import functools

import jax
import jax.numpy as jnp
import ml_dtypes
import numpy as np
from jax import lax
from jax.experimental import pallas as pl
from jax.experimental.pallas import tpu as pltpu
from jax.sharding import PartitionSpec as P

MESH = pl.DeviceIdType.MESH
BF16 = jnp.bfloat16
F32 = jnp.float32


def split_table(table, axis):
    high = table.astype(ml_dtypes.bfloat16)
    low = (table - high.astype(np.float64)).astype(ml_dtypes.bfloat16)
    return np.concatenate([high, low], axis=axis)


def make_tables(blocks, width):
    a = np.arange(blocks)[:, None]
    c = np.arange(blocks)[None, :] + 0.5
    phase = 2 * np.pi * a * c / (2 * blocks)
    first = split_table(np.concatenate([np.cos(phase).T, -np.sin(phase).T], axis=0), 1)
    last = split_table(np.concatenate([np.cos(phase), -np.sin(phase)], axis=1), 1)
    b = np.arange(width)
    turn = 2 * np.pi * c.T * b[None, :] / (2 * blocks * width)
    twist = np.concatenate([np.cos(turn), np.sin(turn)], axis=0).astype(np.float32)
    angle = 2 * np.pi * ((b[:, None] * b[None, :]) % width) / width
    cos, sin = np.cos(angle), np.sin(angle)
    forth = np.block([[cos, -sin], [sin, cos]]).astype(ml_dtypes.bfloat16)
    back = np.block([[cos, sin], [-sin, cos]]).astype(ml_dtypes.bfloat16)
    return first, last, twist, forth, back


def dot(x, y):
    return jnp.dot(x, y, preferred_element_type=F32)


def kernel(
    blocks, count, width,
    k_hbm, v_hbm, g_hbm, q_hbm, taps_hbm, skip_hbm, first_hbm, last_hbm, twist_hbm, forth_hbm, back_hbm,
    q_hbm_out, k_hbm_out, v_hbm_out, tap_out,
    q_out, k_out, v_out, k_in, v_in, g_in, q_in, taps_in, skip_in, first, last, twist, forth, back,
    sent, arrived, returned, packed, wide, gated_spec, taps_spec, prod_spec, mixed,
    load_sem, store_sem, own_sem, send_sem, recv_sem,
):
    me = lax.axis_index("ctx")
    rows = blocks * count
    lanes = 128
    halves = width // lanes
    loads = [
        pltpu.make_async_copy(src, dst, load_sem.at[i])
        for i, (src, dst) in enumerate(
            (
                (k_hbm, k_in), (v_hbm, v_in), (taps_hbm, taps_in), (g_hbm, g_in), (q_hbm, q_in),
                (skip_hbm, skip_in), (first_hbm, first), (last_hbm, last), (twist_hbm, twist), (forth_hbm, forth), (back_hbm, back),
            )
        )
    ]
    for load in loads:
        load.start()

    barrier = pltpu.get_barrier_semaphore()

    def greet(j, carry):
        peer = lax.rem(me + j, blocks)
        pl.semaphore_signal(barrier, inc=1, device_id={"ctx": peer}, device_id_type=MESH)
        return carry

    lax.fori_loop(1, blocks, greet, 0)

    def own_rows():
        return pl.ds(pl.multiple_of(me * count, count), count)

    def send(i, target):
        def one(j, carry):
            peer = lax.rem(me + j, blocks)
            pltpu.make_async_remote_copy(
                src_ref=sent.at[i, pl.ds(pl.multiple_of(peer * count, count), count)],
                dst_ref=target.at[own_rows()],
                send_sem=send_sem.at[i],
                recv_sem=recv_sem.at[i],
                device_id={"ctx": peer},
                device_id_type=MESH,
            ).start()
            return carry

        lax.fori_loop(1, blocks, one, 0)

    def wait_all(i, target, sem):
        part = pl.ds(0, rows - count)
        pltpu.make_async_copy(target.at[part], target.at[part], sem.at[i]).wait()

    loads[0].wait()
    loads[1].wait()
    sent[0] = (k_in[...].astype(F32) * v_in[...].astype(F32)).astype(BF16)
    pl.semaphore_wait(barrier, blocks - 1)
    send(0, arrived.at[0])
    loads[2].wait()
    sent[1] = taps_in[...].astype(BF16)
    send(1, arrived.at[1])
    loads[3].wait()
    loads[4].wait()
    sent[2] = (g_in[...].astype(F32) * q_in[...].astype(F32)).astype(BF16)
    send(2, arrived.at[2])
    for load in loads[5:]:
        load.wait()

    group = 4
    tile = group * blocks

    def transform(i, spec):
        wait_all(i, arrived.at[i], recv_sem)
        arrived[i, own_rows()] = sent[i, own_rows()]
        for h in range(halves):
            wide[h] = arrived[i, :, lanes * h : lanes * (h + 1)].astype(F32)

        def one(t, carry):
            for s in range(group):
                every = pl.ds(t * group + s, blocks, stride=count)
                x = jnp.concatenate([wide[h, every, :] for h in range(halves)], axis=1).astype(BF16)
                y = dot(first[...], jnp.concatenate([x, x], axis=0))
                real, imag = y[:blocks], y[blocks:]
                cos, sin = twist[:blocks], twist[blocks:]
                packed[s * blocks : (s + 1) * blocks, :width] = (real * cos + imag * sin).astype(BF16)
                packed[s * blocks : (s + 1) * blocks, width:] = (imag * cos - real * sin).astype(BF16)
            spec[pl.ds(pl.multiple_of(t * tile, tile), tile), :] = dot(packed[...], forth[...])
            return carry

        lax.fori_loop(0, count // group, one, 0)

    def multiply_back(i, left, right, conjugate, scale):
        def one(t, carry):
            part = pl.ds(pl.multiple_of(t * tile, tile), tile)
            lr, li = left[part, :width], left[part, width:]
            rr, ri = right[part, :width], right[part, width:]
            if conjugate:
                mixed[:, :width] = (lr * rr + li * ri).astype(BF16)
                mixed[:, width:] = (li * rr - lr * ri).astype(BF16)
            else:
                mixed[:, :width] = (lr * rr - li * ri).astype(BF16)
                mixed[:, width:] = (lr * ri + li * rr).astype(BF16)
            u = dot(mixed[...], back[...])
            cos, sin = twist[:blocks] * scale, twist[blocks:] * scale
            for s in range(group):
                real = u[s * blocks : (s + 1) * blocks, :width]
                imag = u[s * blocks : (s + 1) * blocks, width:]
                turned = jnp.concatenate(
                    [(real * cos - imag * sin).astype(BF16), (imag * cos + real * sin).astype(BF16)], axis=0
                )
                out = dot(last[...], jnp.concatenate([turned, turned], axis=0))
                for h in range(halves):
                    wide[h, pl.ds(t * group + s, blocks, stride=count), :] = out[:, lanes * h : lanes * (h + 1)]
            return carry

        lax.fori_loop(0, count // group, one, 0)
        for h in range(halves):
            sent[i, :, lanes * h : lanes * (h + 1)] = wide[h].astype(BF16)

    def give(i, target):
        send(i, target)
        target[own_rows()] = sent[i, own_rows()]

    norm = 1.0 / (blocks * width)
    fwd, bwd = returned.at[0], returned.at[1]
    transform(0, gated_spec)
    transform(1, taps_spec)
    multiply_back(3, gated_spec, taps_spec, False, norm)
    give(3, fwd)
    transform(2, prod_spec)
    multiply_back(4, prod_spec, taps_spec, True, norm)
    give(4, bwd)
    multiply_back(5, prod_spec, gated_spec, True, norm * (blocks * width) ** -0.5)
    own_taps = pltpu.make_async_copy(sent.at[5, own_rows()], tap_out.at[own_rows()], own_sem)
    own_taps.start()
    send(5, tap_out)

    skip_cols = skip_in[...].T

    def each_part(body):
        for s in range(rows // lanes):
            body(pl.ds(s * lanes, lanes), skip_cols[:, s : s + 1])

    def finish_q(part, skip):
        total = returned[0, part].astype(F32) + skip * sent[0, part].astype(F32)
        q_out[part] = (g_in[part].astype(F32) * total).astype(BF16)

    def finish_kv(part, skip):
        z_grad = returned[1, part].astype(F32) + skip * sent[2, part].astype(F32)
        k_out[part] = (v_in[part].astype(F32) * z_grad).astype(BF16)
        v_out[part] = (k_in[part].astype(F32) * z_grad).astype(BF16)

    stores = [
        pltpu.make_async_copy(src, dst, store_sem.at[i])
        for i, (src, dst) in enumerate(((q_out, q_hbm_out), (k_out, k_hbm_out), (v_out, v_hbm_out)))
    ]
    wait_all(3, fwd, recv_sem)
    each_part(finish_q)
    stores[0].start()
    wait_all(4, bwd, recv_sem)
    each_part(finish_kv)
    stores[1].start()
    stores[2].start()
    own_taps.wait()
    for store in stores:
        store.wait()
    for i in range(6):
        wait_all(i, sent.at[i], send_sem)
    wait_all(5, tap_out, recv_sem)


def store_kernel(q_ref, k_ref, v_ref, tap_ref, q_out, k_out, v_out, tap_out, held, wide, sems):
    parts = 2
    step = wide.shape[0] // parts
    moves = []
    for i, (src, dst) in enumerate(((tap_ref, tap_out), (q_ref, q_out), (k_ref, k_out), (v_ref, v_out))):
        for p in range(parts):
            rows = pl.ds(p * step, step)
            stage = wide.at[rows] if i == 0 else held.at[i, rows]
            load = pltpu.make_async_copy(src.at[rows], held.at[i, rows], sems.at[0, i, p])
            store = pltpu.make_async_copy(stage, dst.at[rows], sems.at[1, i, p])
            load.start()
            moves.append((load, store, i, rows))
    for load, store, i, rows in moves:
        load.wait()
        if i == 0:
            wide[rows] = held[0, rows].astype(F32)
        store.start()
    for _, store, _, _ in moves:
        store.wait()


def exchange_convolve(k_field, v_field, out_grad, q_field, taps, skip, blocks):
    channels, width = k_field.shape
    count = channels // blocks
    rows = channels
    lanes = 128
    tables = make_tables(blocks, width)
    hbm = pl.BlockSpec(memory_space=pltpu.HBM)
    field = pltpu.VMEM((rows, width), BF16)
    spectrum = pltpu.VMEM((rows, 2 * width), F32)
    table_space = [pltpu.VMEM(t.shape, t.dtype) for t in tables]
    dma = pltpu.SemaphoreType.DMA
    result = jax.ShapeDtypeStruct((rows, width), BF16)
    grads = pl.pallas_call(
        functools.partial(kernel, blocks, count, width),
        out_shape=[result] * 4,
        in_specs=[hbm] * 11,
        out_specs=[hbm] * 4,
        scratch_shapes=[
            field, field, field, field, field, field, field,
            pltpu.VMEM((rows, width), F32), pltpu.VMEM((rows // lanes, lanes), F32), *table_space,
            pltpu.VMEM((6, rows, width), BF16),
            pltpu.VMEM((3, rows, width), BF16),
            pltpu.VMEM((2, rows, width), BF16),
            pltpu.VMEM((4 * blocks, 2 * width), BF16),
            pltpu.VMEM((width // lanes, rows, lanes), F32),
            spectrum, spectrum, spectrum,
            pltpu.VMEM((4 * blocks, 2 * width), BF16),
            dma((11,)), dma((3,)), dma, dma((6,)), dma((6,)),
        ],
        compiler_params=pltpu.CompilerParams(
            collective_id=0, has_side_effects=True, vmem_limit_bytes=58 * 2**20
        ),
        name="exchange_convolve",
    )(
        k_field, v_field, out_grad, q_field, taps, skip.reshape(rows // lanes, lanes),
        *[jnp.asarray(t) for t in tables],
    )
    return pl.pallas_call(
        store_kernel,
        out_shape=[result] * 3 + [jax.ShapeDtypeStruct((rows, width), F32)],
        in_specs=[hbm] * 4,
        out_specs=[hbm] * 4,
        scratch_shapes=[pltpu.VMEM((4, rows, width), BF16), pltpu.VMEM((rows, width), F32), dma((2, 4, 2))],
        compiler_params=pltpu.CompilerParams(vmem_limit_bytes=58 * 2**20),
        name="store_grads",
    )(*grads)


def local(blocks, q_field, k_field, v_field, out_grad, filter_taps, skip):
    return tuple(exchange_convolve(k_field, v_field, out_grad, q_field, filter_taps, skip, blocks))


def solution(mesh):
    spec = P("tp", "ctx")
    return jax.shard_map(
        functools.partial(local, mesh.shape["ctx"]),
        mesh=mesh,
        in_specs=(spec, spec, spec, spec, spec, P("tp")),
        out_specs=(spec, spec, spec, spec),
        check_vma=False,
    )
```

```python
import functools

import jax
import jax.numpy as jnp
import ml_dtypes
import numpy as np
from jax import lax
from jax.experimental import pallas as pl
from jax.experimental.pallas import tpu as pltpu
from jax.sharding import PartitionSpec as P

MESH = pl.DeviceIdType.MESH
BF16 = jnp.bfloat16
F32 = jnp.float32


def split_table(table, axis):
    high = table.astype(ml_dtypes.bfloat16)
    low = (table - high.astype(np.float64)).astype(ml_dtypes.bfloat16)
    return np.concatenate([high, low], axis=axis)


def make_tables(blocks, width):
    a = np.arange(blocks)[:, None]
    c = np.arange(blocks)[None, :] + 0.5
    phase = 2 * np.pi * a * c / (2 * blocks)
    first = split_table(np.concatenate([np.cos(phase).T, -np.sin(phase).T], axis=0), 1)
    last = split_table(np.concatenate([np.cos(phase), -np.sin(phase)], axis=1), 1)
    b = np.arange(width)
    turn = 2 * np.pi * c.T * b[None, :] / (2 * blocks * width)
    twist = np.concatenate([np.cos(turn), np.sin(turn)], axis=0).astype(np.float32)
    angle = 2 * np.pi * ((b[:, None] * b[None, :]) % width) / width
    cos, sin = np.cos(angle), np.sin(angle)
    forth = np.block([[cos, -sin], [sin, cos]]).astype(ml_dtypes.bfloat16)
    back = np.block([[cos, sin], [-sin, cos]]).astype(ml_dtypes.bfloat16)
    return first, last, twist, forth, back


def dot(x, y):
    return jnp.dot(x, y, preferred_element_type=F32)


def kernel(
    blocks, count, width,
    k_hbm, v_hbm, g_hbm, q_hbm, taps_hbm, skip_hbm, first_hbm, last_hbm, twist_hbm, forth_hbm, back_hbm,
    q_hbm_out, k_hbm_out, v_hbm_out, tap_out,
    q_out, k_out, v_out, k_in, v_in, g_in, q_in, taps_in, skip_in, first, last, twist, forth, back,
    sent, crossed, arrived, returned, packed, wide, gated_spec, taps_spec, prod_spec, mixed,
    load_sem, store_sem, own_sem, ready, cross_send, cross_recv, plane_send, plane_recv,
):
    me = lax.axis_index("ctx")
    half = blocks // 2
    z = lax.rem(lax.div(me, 2), 2)
    i = 2 * lax.div(me, 4) + lax.rem(me, 2)
    partner = me + 2 - 4 * z
    rows = blocks * count
    side = half * count
    lanes = 128
    halves = width // lanes
    loads = [
        pltpu.make_async_copy(src, dst, load_sem.at[n])
        for n, (src, dst) in enumerate(
            (
                (k_hbm, k_in), (v_hbm, v_in), (taps_hbm, taps_in), (g_hbm, g_in), (q_hbm, q_in),
                (skip_hbm, skip_in), (first_hbm, first), (last_hbm, last), (twist_hbm, twist), (forth_hbm, forth), (back_hbm, back),
            )
        )
    ]
    for load in loads[:2]:
        load.start()

    def block(index):
        return pl.ds(pl.multiple_of(index * count, count), count)

    def part_of(which):
        return pl.ds(pl.multiple_of(which * side, side), side)

    def plane_device(k):
        place = lax.rem(i + k, half)
        return place, 4 * lax.div(place, 2) + 2 * z + lax.rem(place, 2)

    barrier = pltpu.get_barrier_semaphore()
    pl.semaphore_signal(barrier, inc=1, device_id={"ctx": partner}, device_id_type=MESH)

    def greet(k, carry):
        _, peer = plane_device(k)
        pl.semaphore_signal(barrier, inc=1, device_id={"ctx": peer}, device_id_type=MESH)
        return carry

    lax.fori_loop(1, half, greet, 0)
    for load in loads[2:]:
        load.start()

    def cross(src, dst):
        pltpu.make_async_remote_copy(
            src_ref=src, dst_ref=dst, send_sem=cross_send, recv_sem=cross_recv,
            device_id={"ctx": partner}, device_id_type=MESH,
        ).start()

    def in_plane(n, moves):
        def one(k, carry):
            place, peer = plane_device(k)
            for slot, src, dst in moves(place, peer):
                pltpu.make_async_remote_copy(
                    src_ref=src, dst_ref=dst, send_sem=plane_send.at[n], recv_sem=plane_recv.at[slot],
                    device_id={"ctx": peer}, device_id_type=MESH,
                ).start()
            return carry

        lax.fori_loop(1, half, one, 0)

    def wait_rows(ref, n_rows, sem):
        part = ref.at[pl.ds(0, n_rows)]
        pltpu.make_async_copy(part, part, sem).wait()

    def send_own(n):
        in_plane(n, lambda place, peer: [(n, sent.at[n, block(z * half + place)], arrived.at[n, block(me)])])
        arrived[n, block(me)] = sent[n, block(z * half + i)]

    def send_on(n):
        wait_rows(crossed, side, cross_recv)
        in_plane(n, lambda place, peer: [(n, crossed.at[block(place)], arrived.at[n, block(partner)])])
        arrived[n, block(partner)] = crossed[block(i)]

    def to_all(n, recv, source, dst):
        def one(k, carry):
            peer = lax.rem(me + k, blocks)
            pltpu.make_async_remote_copy(
                src_ref=source(peer), dst_ref=dst, send_sem=plane_send.at[n], recv_sem=plane_recv.at[recv],
                device_id={"ctx": peer}, device_id_type=MESH,
            ).start()
            return carry

        lax.fori_loop(1, blocks, one, 0)

    def owner_block(device):
        return block(lax.rem(lax.div(device, 2), 2) * half + 2 * lax.div(device, 4) + lax.rem(device, 2))

    def send_direct(n):
        to_all(n, n, lambda peer: sent.at[n, owner_block(peer)], arrived.at[n, block(me)])
        arrived[n, block(me)] = sent[n, owner_block(me)]

    def give(n, target):
        to_all(n, n, lambda peer: sent.at[n, block(peer)], target.at[owner_block(me)])

    loads[0].wait()
    loads[1].wait()
    sent[0] = (k_in[...].astype(F32) * v_in[...].astype(F32)).astype(BF16)
    pl.semaphore_wait(barrier, half)
    cross(sent.at[0, part_of(1 - z)], crossed)
    pl.semaphore_signal(ready, inc=1, device_id={"ctx": partner}, device_id_type=MESH)
    send_own(0)
    loads[2].wait()
    sent[1] = taps_in[...].astype(BF16)
    loads[3].wait()
    loads[4].wait()
    sent[2] = (g_in[...].astype(F32) * q_in[...].astype(F32)).astype(BF16)
    pl.semaphore_wait(ready, 1)
    send_direct(1)
    send_direct(2)
    for load in loads[5:]:
        load.wait()

    group = 4
    tile = group * blocks

    def transform(n, spec):
        wait_rows(arrived.at[n], rows - (2 if n == 0 else 1) * count, plane_recv.at[n])
        for h in range(halves):
            wide[h] = arrived[n, :, lanes * h : lanes * (h + 1)].astype(F32)

        def one(t, carry):
            for s in range(group):
                every = pl.ds(t * group + s, blocks, stride=count)
                x = jnp.concatenate([wide[h, every, :] for h in range(halves)], axis=1).astype(BF16)
                y = dot(first[...], jnp.concatenate([x, x], axis=0))
                real, imag = y[:blocks], y[blocks:]
                cos, sin = twist[:blocks], twist[blocks:]
                packed[s * blocks : (s + 1) * blocks, :width] = (real * cos + imag * sin).astype(BF16)
                packed[s * blocks : (s + 1) * blocks, width:] = (imag * cos - real * sin).astype(BF16)
            spec[pl.ds(pl.multiple_of(t * tile, tile), tile), :] = dot(packed[...], forth[...])
            return carry

        lax.fori_loop(0, count // group, one, 0)

    def multiply_back(n, left, right, conjugate, scale):
        def one(t, carry):
            part = pl.ds(pl.multiple_of(t * tile, tile), tile)
            lr, li = left[part, :width], left[part, width:]
            rr, ri = right[part, :width], right[part, width:]
            if conjugate:
                mixed[:, :width] = (lr * rr + li * ri).astype(BF16)
                mixed[:, width:] = (li * rr - lr * ri).astype(BF16)
            else:
                mixed[:, :width] = (lr * rr - li * ri).astype(BF16)
                mixed[:, width:] = (lr * ri + li * rr).astype(BF16)
            u = dot(mixed[...], back[...])
            cos, sin = twist[:blocks] * scale, twist[blocks:] * scale
            for s in range(group):
                real = u[s * blocks : (s + 1) * blocks, :width]
                imag = u[s * blocks : (s + 1) * blocks, width:]
                turned = jnp.concatenate(
                    [(real * cos - imag * sin).astype(BF16), (imag * cos + real * sin).astype(BF16)], axis=0
                )
                out = dot(last[...], jnp.concatenate([turned, turned], axis=0))
                for h in range(halves):
                    wide[h, pl.ds(t * group + s, blocks, stride=count), :] = out[:, lanes * h : lanes * (h + 1)]
            return carry

        lax.fori_loop(0, count // group, one, 0)
        for h in range(halves):
            sent[n, :, lanes * h : lanes * (h + 1)] = wide[h].astype(BF16)

    norm = 1.0 / (blocks * width)
    fwd, bwd = returned.at[0], returned.at[1]
    send_on(0)
    transform(0, gated_spec)
    transform(1, taps_spec)
    multiply_back(3, gated_spec, taps_spec, False, norm)
    give(3, fwd)
    fwd[owner_block(me)] = sent[3, block(me)]
    transform(2, prod_spec)
    multiply_back(4, prod_spec, taps_spec, True, norm)
    give(4, bwd)
    bwd[owner_block(me)] = sent[4, block(me)]
    multiply_back(5, prod_spec, gated_spec, True, norm * (blocks * width) ** -0.5)
    give(5, tap_out)
    own_taps = pltpu.make_async_copy(sent.at[5, block(me)], tap_out.at[owner_block(me)], own_sem)
    own_taps.start()

    skip_cols = skip_in[...].T

    def each_part(body):
        for s in range(rows // lanes):
            body(pl.ds(s * lanes, lanes), skip_cols[:, s : s + 1])

    def finish_q(part, skip):
        total = returned[0, part].astype(F32) + skip * sent[0, part].astype(F32)
        q_out[part] = (g_in[part].astype(F32) * total).astype(BF16)

    def finish_kv(part, skip):
        z_grad = returned[1, part].astype(F32) + skip * sent[2, part].astype(F32)
        k_out[part] = (v_in[part].astype(F32) * z_grad).astype(BF16)
        v_out[part] = (k_in[part].astype(F32) * z_grad).astype(BF16)

    stores = [
        pltpu.make_async_copy(src, dst, store_sem.at[n])
        for n, (src, dst) in enumerate(((q_out, q_hbm_out), (k_out, k_hbm_out), (v_out, v_hbm_out)))
    ]
    wait_rows(fwd, rows - count, plane_recv.at[3])
    each_part(finish_q)
    stores[0].start()
    wait_rows(bwd, rows - count, plane_recv.at[4])
    each_part(finish_kv)
    stores[1].start()
    stores[2].start()
    own_taps.wait()
    for store in stores:
        store.wait()
    wait_rows(crossed, side, cross_send)
    for n in range(6):
        wait_rows(sent.at[n], rows - (2 if n == 0 else 1) * count, plane_send.at[n])
    wait_rows(tap_out, rows - count, plane_recv.at[5])


def store_kernel(q_ref, k_ref, v_ref, tap_ref, q_out, k_out, v_out, tap_out, held, wide, sems):
    parts = 2
    step = wide.shape[0] // parts
    moves = []
    for i, (src, dst) in enumerate(((tap_ref, tap_out), (q_ref, q_out), (k_ref, k_out), (v_ref, v_out))):
        for p in range(parts):
            rows = pl.ds(p * step, step)
            stage = wide.at[rows] if i == 0 else held.at[i, rows]
            load = pltpu.make_async_copy(src.at[rows], held.at[i, rows], sems.at[0, i, p])
            store = pltpu.make_async_copy(stage, dst.at[rows], sems.at[1, i, p])
            load.start()
            moves.append((load, store, i, rows))
    for load, store, i, rows in moves:
        load.wait()
        if i == 0:
            wide[rows] = held[0, rows].astype(F32)
        store.start()
    for _, store, _, _ in moves:
        store.wait()


def exchange_convolve(k_field, v_field, out_grad, q_field, taps, skip, blocks):
    channels, width = k_field.shape
    count = channels // blocks
    rows = channels
    lanes = 128
    tables = make_tables(blocks, width)
    hbm = pl.BlockSpec(memory_space=pltpu.HBM)
    field = pltpu.VMEM((rows, width), BF16)
    spectrum = pltpu.VMEM((rows, 2 * width), F32)
    table_space = [pltpu.VMEM(t.shape, t.dtype) for t in tables]
    dma = pltpu.SemaphoreType.DMA
    result = jax.ShapeDtypeStruct((rows, width), BF16)
    grads = pl.pallas_call(
        functools.partial(kernel, blocks, count, width),
        out_shape=[result] * 4,
        in_specs=[hbm] * 11,
        out_specs=[hbm] * 4,
        scratch_shapes=[
            field, field, field, field, field, field, field,
            pltpu.VMEM((rows, width), F32), pltpu.VMEM((rows // lanes, lanes), F32), *table_space,
            pltpu.VMEM((6, rows, width), BF16),
            pltpu.VMEM((rows // 2, width), BF16),
            pltpu.VMEM((3, rows, width), BF16),
            pltpu.VMEM((2, rows, width), BF16),
            pltpu.VMEM((4 * blocks, 2 * width), BF16),
            pltpu.VMEM((width // lanes, rows, lanes), F32),
            spectrum, spectrum, spectrum,
            pltpu.VMEM((4 * blocks, 2 * width), BF16),
            dma((11,)), dma((3,)), dma, pltpu.SemaphoreType.REGULAR, dma, dma, dma((6,)), dma((6,)),
        ],
        compiler_params=pltpu.CompilerParams(
            collective_id=0, has_side_effects=True, vmem_limit_bytes=58 * 2**20
        ),
        name="exchange_convolve",
    )(
        k_field, v_field, out_grad, q_field, taps, skip.reshape(rows // lanes, lanes),
        *[jnp.asarray(t) for t in tables],
    )
    return pl.pallas_call(
        store_kernel,
        out_shape=[result] * 3 + [jax.ShapeDtypeStruct((rows, width), F32)],
        in_specs=[hbm] * 4,
        out_specs=[hbm] * 4,
        scratch_shapes=[pltpu.VMEM((4, rows, width), BF16), pltpu.VMEM((rows, width), F32), dma((2, 4, 2))],
        compiler_params=pltpu.CompilerParams(vmem_limit_bytes=58 * 2**20),
        name="store_grads",
    )(*grads)


def local(blocks, q_field, k_field, v_field, out_grad, filter_taps, skip):
    return tuple(exchange_convolve(k_field, v_field, out_grad, q_field, filter_taps, skip, blocks))


def solution(mesh):
    spec = P("tp", "ctx")
    return jax.shard_map(
        functools.partial(local, mesh.shape["ctx"]),
        mesh=mesh,
        in_specs=(spec, spec, spec, spec, spec, P("tp")),
        out_specs=(spec, spec, spec, spec),
        check_vma=False,
    )
```

```python
import functools

import jax
import jax.numpy as jnp
import ml_dtypes
import numpy as np
from jax import lax
from jax.experimental import pallas as pl
from jax.experimental.pallas import tpu as pltpu
from jax.sharding import PartitionSpec as P

MESH = pl.DeviceIdType.MESH
BF16 = jnp.bfloat16
F32 = jnp.float32


def split_table(table):
    high = table.astype(ml_dtypes.bfloat16)
    return high, (table - high.astype(np.float64)).astype(ml_dtypes.bfloat16)


def split(x):
    high = x.astype(BF16)
    return high, (x - high.astype(F32)).astype(BF16)


def make_tables(blocks, width):
    a = np.arange(blocks)[:, None]
    c = np.arange(blocks)[None, :] + 0.5
    phase = 2 * np.pi * a * c / (2 * blocks)
    first = np.concatenate(split_table(np.concatenate([np.cos(phase).T, -np.sin(phase).T], axis=0)), axis=1)
    high, low = split_table(np.concatenate([np.cos(phase), -np.sin(phase)], axis=1))
    last = np.concatenate([high, low, high], axis=1)
    b = np.arange(width)
    turn = 2 * np.pi * c.T * b[None, :] / (2 * blocks * width)
    twist = np.concatenate([np.cos(turn), np.sin(turn)], axis=0).astype(np.float32)
    angle = 2 * np.pi * ((b[:, None] * b[None, :]) % width) / width
    cos, sin = np.cos(angle), np.sin(angle)
    forth = np.stack(split_table(np.block([[cos, -sin], [sin, cos]])))
    back = np.stack(split_table(np.block([[cos, sin], [-sin, cos]])))
    return first, last, twist, forth, back


def dot(x, y):
    return jnp.dot(x, y, preferred_element_type=F32)


def dot_split(x, table):
    return dot(
        jnp.concatenate([x[0], x[0], x[1]], axis=1), jnp.concatenate([table[0], table[1], table[0]], axis=0)
    )


def kernel(
    blocks, count, width,
    k_hbm, v_hbm, g_hbm, q_hbm, taps_hbm, skip_hbm, first_hbm, last_hbm, twist_hbm, forth_hbm, back_hbm,
    q_hbm_out, k_hbm_out, v_hbm_out, tap_out,
    q_out, k_out, v_out, k_in, v_in, g_in, q_in, taps_in, skip_in, first, last, twist, forth, back,
    sent, crossed, arrived, returned, packed, wide, gated_spec, taps_spec, prod_spec, mixed,
    load_sem, store_sem, own_sem, ready, cross_send, cross_recv, plane_send, plane_recv,
):
    me = lax.axis_index("ctx")
    half = blocks // 2
    z = lax.rem(lax.div(me, 2), 2)
    i = 2 * lax.div(me, 4) + lax.rem(me, 2)
    partner = me + 2 - 4 * z
    rows = blocks * count
    side = half * count
    lanes = 128
    halves = width // lanes
    loads = [
        pltpu.make_async_copy(src, dst, load_sem.at[n])
        for n, (src, dst) in enumerate(
            (
                (k_hbm, k_in), (v_hbm, v_in), (taps_hbm, taps_in), (g_hbm, g_in), (q_hbm, q_in),
                (skip_hbm, skip_in), (first_hbm, first), (last_hbm, last), (twist_hbm, twist), (forth_hbm, forth), (back_hbm, back),
            )
        )
    ]
    for load in loads[:2]:
        load.start()

    def block(index):
        return pl.ds(pl.multiple_of(index * count, count), count)

    def part_of(which):
        return pl.ds(pl.multiple_of(which * side, side), side)

    def plane_device(k):
        place = lax.rem(i + k, half)
        return place, 4 * lax.div(place, 2) + 2 * z + lax.rem(place, 2)

    barrier = pltpu.get_barrier_semaphore()
    pl.semaphore_signal(barrier, inc=1, device_id={"ctx": partner}, device_id_type=MESH)

    def greet(k, carry):
        _, peer = plane_device(k)
        pl.semaphore_signal(barrier, inc=1, device_id={"ctx": peer}, device_id_type=MESH)
        return carry

    lax.fori_loop(1, half, greet, 0)
    for load in loads[2:]:
        load.start()

    def cross(src, dst):
        pltpu.make_async_remote_copy(
            src_ref=src, dst_ref=dst, send_sem=cross_send, recv_sem=cross_recv,
            device_id={"ctx": partner}, device_id_type=MESH,
        ).start()

    def in_plane(n, moves):
        def one(k, carry):
            place, peer = plane_device(k)
            for slot, src, dst in moves(place, peer):
                pltpu.make_async_remote_copy(
                    src_ref=src, dst_ref=dst, send_sem=plane_send.at[n], recv_sem=plane_recv.at[slot],
                    device_id={"ctx": peer}, device_id_type=MESH,
                ).start()
            return carry

        lax.fori_loop(1, half, one, 0)

    def wait_rows(ref, n_rows, sem):
        part = ref.at[pl.ds(0, n_rows)]
        pltpu.make_async_copy(part, part, sem).wait()

    def send_own(n):
        in_plane(n, lambda place, peer: [(n, sent.at[n, block(z * half + place)], arrived.at[n, block(me)])])
        arrived[n, block(me)] = sent[n, block(z * half + i)]

    def send_on(n):
        wait_rows(crossed, side, cross_recv)
        in_plane(n, lambda place, peer: [(n, crossed.at[block(place)], arrived.at[n, block(partner)])])
        arrived[n, block(partner)] = crossed[block(i)]

    def to_all(n, recv, source, dst):
        def one(k, carry):
            peer = lax.rem(me + k, blocks)
            pltpu.make_async_remote_copy(
                src_ref=source(peer), dst_ref=dst, send_sem=plane_send.at[n], recv_sem=plane_recv.at[recv],
                device_id={"ctx": peer}, device_id_type=MESH,
            ).start()
            return carry

        lax.fori_loop(1, blocks, one, 0)

    def owner_block(device):
        return block(lax.rem(lax.div(device, 2), 2) * half + 2 * lax.div(device, 4) + lax.rem(device, 2))

    def send_direct(n):
        to_all(n, n, lambda peer: sent.at[n, owner_block(peer)], arrived.at[n, block(me)])
        arrived[n, block(me)] = sent[n, owner_block(me)]

    def give(n, target):
        to_all(n, n, lambda peer: sent.at[n, block(peer)], target.at[owner_block(me)])

    loads[0].wait()
    loads[1].wait()
    sent[0] = (k_in[...].astype(F32) * v_in[...].astype(F32)).astype(BF16)
    pl.semaphore_wait(barrier, half)
    cross(sent.at[0, part_of(1 - z)], crossed)
    pl.semaphore_signal(ready, inc=1, device_id={"ctx": partner}, device_id_type=MESH)
    send_own(0)
    loads[2].wait()
    sent[1] = taps_in[...].astype(BF16)
    loads[3].wait()
    loads[4].wait()
    sent[2] = (g_in[...].astype(F32) * q_in[...].astype(F32)).astype(BF16)
    pl.semaphore_wait(ready, 1)
    send_direct(1)
    send_direct(2)
    for load in loads[5:]:
        load.wait()

    group = 4
    tile = group * blocks

    def transform(n, spec):
        wait_rows(arrived.at[n], rows - (2 if n == 0 else 1) * count, plane_recv.at[n])
        for h in range(halves):
            wide[h] = arrived[n, :, lanes * h : lanes * (h + 1)].astype(F32)

        def one(t, carry):
            for s in range(group):
                every = pl.ds(t * group + s, blocks, stride=count)
                x = jnp.concatenate([wide[h, every, :] for h in range(halves)], axis=1).astype(BF16)
                y = dot(first[...], jnp.concatenate([x, x], axis=0))
                real, imag = y[:blocks], y[blocks:]
                cos, sin = twist[:blocks], twist[blocks:]
                part = slice(s * blocks, (s + 1) * blocks)
                packed[0, part, :width], packed[1, part, :width] = split(real * cos + imag * sin)
                packed[0, part, width:], packed[1, part, width:] = split(imag * cos - real * sin)
            spec[pl.ds(pl.multiple_of(t * tile, tile), tile), :] = dot_split(packed, forth)
            return carry

        lax.fori_loop(0, count // group, one, 0)

    def multiply_back(n, left, right, conjugate, scale):
        def one(t, carry):
            part = pl.ds(pl.multiple_of(t * tile, tile), tile)
            lr, li = left[part, :width], left[part, width:]
            rr, ri = right[part, :width], right[part, width:]
            if conjugate:
                mixed[0, :, :width], mixed[1, :, :width] = split(lr * rr + li * ri)
                mixed[0, :, width:], mixed[1, :, width:] = split(li * rr - lr * ri)
            else:
                mixed[0, :, :width], mixed[1, :, :width] = split(lr * rr - li * ri)
                mixed[0, :, width:], mixed[1, :, width:] = split(lr * ri + li * rr)
            u = dot_split(mixed, back)
            cos, sin = twist[:blocks] * scale, twist[blocks:] * scale
            for s in range(group):
                real = u[s * blocks : (s + 1) * blocks, :width]
                imag = u[s * blocks : (s + 1) * blocks, width:]
                high, low = split(jnp.concatenate([real * cos - imag * sin, imag * cos + real * sin], axis=0))
                out = dot(last[...], jnp.concatenate([high, high, low], axis=0))
                for h in range(halves):
                    wide[h, pl.ds(t * group + s, blocks, stride=count), :] = out[:, lanes * h : lanes * (h + 1)]
            return carry

        lax.fori_loop(0, count // group, one, 0)
        for h in range(halves):
            sent[n, :, lanes * h : lanes * (h + 1)] = wide[h].astype(BF16)

    norm = 1.0 / (blocks * width)
    fwd, bwd = returned.at[0], returned.at[1]
    send_on(0)
    transform(0, gated_spec)
    transform(1, taps_spec)
    multiply_back(3, gated_spec, taps_spec, False, norm)
    give(3, fwd)
    fwd[owner_block(me)] = sent[3, block(me)]
    transform(2, prod_spec)
    multiply_back(4, prod_spec, taps_spec, True, norm)
    give(4, bwd)
    bwd[owner_block(me)] = sent[4, block(me)]
    multiply_back(5, prod_spec, gated_spec, True, norm * (blocks * width) ** -0.5)
    give(5, tap_out)
    own_taps = pltpu.make_async_copy(sent.at[5, block(me)], tap_out.at[owner_block(me)], own_sem)
    own_taps.start()

    skip_cols = skip_in[...].T

    def each_part(body):
        for s in range(rows // lanes):
            body(pl.ds(s * lanes, lanes), skip_cols[:, s : s + 1])

    def finish_q(part, skip):
        total = returned[0, part].astype(F32) + skip * sent[0, part].astype(F32)
        q_out[part] = (g_in[part].astype(F32) * total).astype(BF16)

    def finish_kv(part, skip):
        z_grad = returned[1, part].astype(F32) + skip * sent[2, part].astype(F32)
        k_out[part] = (v_in[part].astype(F32) * z_grad).astype(BF16)
        v_out[part] = (k_in[part].astype(F32) * z_grad).astype(BF16)

    stores = [
        pltpu.make_async_copy(src, dst, store_sem.at[n])
        for n, (src, dst) in enumerate(((q_out, q_hbm_out), (k_out, k_hbm_out), (v_out, v_hbm_out)))
    ]
    wait_rows(fwd, rows - count, plane_recv.at[3])
    each_part(finish_q)
    stores[0].start()
    wait_rows(bwd, rows - count, plane_recv.at[4])
    each_part(finish_kv)
    stores[1].start()
    stores[2].start()
    own_taps.wait()
    for store in stores:
        store.wait()
    wait_rows(crossed, side, cross_send)
    for n in range(6):
        wait_rows(sent.at[n], rows - (2 if n == 0 else 1) * count, plane_send.at[n])
    wait_rows(tap_out, rows - count, plane_recv.at[5])


def store_kernel(q_ref, k_ref, v_ref, tap_ref, q_out, k_out, v_out, tap_out, held, wide, sems):
    parts = 2
    step = wide.shape[0] // parts
    moves = []
    for i, (src, dst) in enumerate(((tap_ref, tap_out), (q_ref, q_out), (k_ref, k_out), (v_ref, v_out))):
        for p in range(parts):
            rows = pl.ds(p * step, step)
            stage = wide.at[rows] if i == 0 else held.at[i, rows]
            load = pltpu.make_async_copy(src.at[rows], held.at[i, rows], sems.at[0, i, p])
            store = pltpu.make_async_copy(stage, dst.at[rows], sems.at[1, i, p])
            load.start()
            moves.append((load, store, i, rows))
    for load, store, i, rows in moves:
        load.wait()
        if i == 0:
            wide[rows] = held[0, rows].astype(F32)
        store.start()
    for _, store, _, _ in moves:
        store.wait()


def exchange_convolve(k_field, v_field, out_grad, q_field, taps, skip, blocks):
    channels, width = k_field.shape
    count = channels // blocks
    rows = channels
    lanes = 128
    tables = make_tables(blocks, width)
    hbm = pl.BlockSpec(memory_space=pltpu.HBM)
    field = pltpu.VMEM((rows, width), BF16)
    spectrum = pltpu.VMEM((rows, 2 * width), F32)
    table_space = [pltpu.VMEM(t.shape, t.dtype) for t in tables]
    dma = pltpu.SemaphoreType.DMA
    result = jax.ShapeDtypeStruct((rows, width), BF16)
    grads = pl.pallas_call(
        functools.partial(kernel, blocks, count, width),
        out_shape=[result] * 4,
        in_specs=[hbm] * 11,
        out_specs=[hbm] * 4,
        scratch_shapes=[
            field, field, field, field, field, field, field,
            pltpu.VMEM((rows, width), F32), pltpu.VMEM((rows // lanes, lanes), F32), *table_space,
            pltpu.VMEM((6, rows, width), BF16),
            pltpu.VMEM((rows // 2, width), BF16),
            pltpu.VMEM((3, rows, width), BF16),
            pltpu.VMEM((2, rows, width), BF16),
            pltpu.VMEM((2, 4 * blocks, 2 * width), BF16),
            pltpu.VMEM((width // lanes, rows, lanes), F32),
            spectrum, spectrum, spectrum,
            pltpu.VMEM((2, 4 * blocks, 2 * width), BF16),
            dma((11,)), dma((3,)), dma, pltpu.SemaphoreType.REGULAR, dma, dma, dma((6,)), dma((6,)),
        ],
        compiler_params=pltpu.CompilerParams(
            collective_id=0, has_side_effects=True, vmem_limit_bytes=58 * 2**20
        ),
        name="exchange_convolve",
    )(
        k_field, v_field, out_grad, q_field, taps, skip.reshape(rows // lanes, lanes),
        *[jnp.asarray(t) for t in tables],
    )
    return pl.pallas_call(
        store_kernel,
        out_shape=[result] * 3 + [jax.ShapeDtypeStruct((rows, width), F32)],
        in_specs=[hbm] * 4,
        out_specs=[hbm] * 4,
        scratch_shapes=[pltpu.VMEM((4, rows, width), BF16), pltpu.VMEM((rows, width), F32), dma((2, 4, 2))],
        compiler_params=pltpu.CompilerParams(vmem_limit_bytes=58 * 2**20),
        name="store_grads",
    )(*grads)


def local(blocks, q_field, k_field, v_field, out_grad, filter_taps, skip):
    return tuple(exchange_convolve(k_field, v_field, out_grad, q_field, filter_taps, skip, blocks))


def solution(mesh):
    spec = P("tp", "ctx")
    return jax.shard_map(
        functools.partial(local, mesh.shape["ctx"]),
        mesh=mesh,
        in_specs=(spec, spec, spec, spec, spec, P("tp")),
        out_specs=(spec, spec, spec, spec),
        check_vma=False,
    )
```

```python
import functools

import jax
import jax.numpy as jnp
import ml_dtypes
import numpy as np
from jax import lax
from jax.experimental import pallas as pl
from jax.experimental.pallas import tpu as pltpu
from jax.sharding import PartitionSpec as P

MESH = pl.DeviceIdType.MESH
BF16 = jnp.bfloat16
F32 = jnp.float32


def split_table(table):
    high = table.astype(ml_dtypes.bfloat16)
    return high, (table - high.astype(np.float64)).astype(ml_dtypes.bfloat16)


def split(x):
    high = x.astype(BF16)
    return high, (x - high.astype(F32)).astype(BF16)


def make_tables(blocks, width):
    a = np.arange(blocks)[:, None]
    c = np.arange(blocks)[None, :] + 0.5
    phase = 2 * np.pi * a * c / (2 * blocks)
    first = np.concatenate(split_table(np.concatenate([np.cos(phase).T, -np.sin(phase).T], axis=0)), axis=1)
    high, low = split_table(np.concatenate([np.cos(phase), -np.sin(phase)], axis=1))
    last = np.concatenate([high, low, high], axis=1)
    b = np.arange(width)
    turn = 2 * np.pi * c.T * b[None, :] / (2 * blocks * width)
    twist = np.concatenate([np.cos(turn), np.sin(turn)], axis=0).astype(np.float32)
    angle = 2 * np.pi * ((b[:, None] * b[None, :]) % width) / width
    cos, sin = np.cos(angle), np.sin(angle)
    forth = np.stack(split_table(np.block([[cos, -sin], [sin, cos]])))
    back = np.stack(split_table(np.block([[cos, sin], [-sin, cos]])))
    return first, last, twist, forth, back


def dot(x, y):
    return jnp.dot(x, y, preferred_element_type=F32)


def dot_split(x, table):
    return dot(
        jnp.concatenate([x[0], x[0], x[1]], axis=1), jnp.concatenate([table[0], table[1], table[0]], axis=0)
    )


def kernel(
    blocks, count, width,
    k_hbm, v_hbm, g_hbm, q_hbm, taps_hbm, skip_hbm, first_hbm, last_hbm, twist_hbm, forth_hbm, back_hbm,
    q_hbm_out, k_hbm_out, v_hbm_out, tap_out,
    q_out, k_out, v_out, k_in, v_in, g_in, q_in, taps_in, skip_in, first, last, twist, forth, back,
    sent, crossed, arrived, returned, packed, wide, gated_spec, taps_spec, prod_spec, mixed,
    load_sem, store_sem, own_sem, ready, cross_send, cross_recv, plane_send, plane_recv,
):
    me = lax.axis_index("ctx")
    half = blocks // 2
    z = lax.rem(lax.div(me, 2), 2)
    i = 2 * lax.div(me, 4) + lax.rem(me, 2)
    partner = me + 2 - 4 * z
    rows = blocks * count
    side = half * count
    lanes = 128
    halves = width // lanes
    loads = [
        pltpu.make_async_copy(src, dst, load_sem.at[n])
        for n, (src, dst) in enumerate(
            (
                (k_hbm, k_in), (v_hbm, v_in), (taps_hbm, taps_in), (g_hbm, g_in), (q_hbm, q_in),
                (skip_hbm, skip_in), (first_hbm, first), (last_hbm, last), (twist_hbm, twist), (forth_hbm, forth), (back_hbm, back),
            )
        )
    ]
    for load in loads[:2]:
        load.start()

    def block(index):
        return pl.ds(pl.multiple_of(index * count, count), count)

    def part_of(which):
        return pl.ds(pl.multiple_of(which * side, side), side)

    def plane_device(k):
        place = lax.rem(i + k, half)
        return place, 4 * lax.div(place, 2) + 2 * z + lax.rem(place, 2)

    barrier = pltpu.get_barrier_semaphore()
    pl.semaphore_signal(barrier, inc=1, device_id={"ctx": partner}, device_id_type=MESH)

    def greet(k, carry):
        _, peer = plane_device(k)
        pl.semaphore_signal(barrier, inc=1, device_id={"ctx": peer}, device_id_type=MESH)
        return carry

    lax.fori_loop(1, half, greet, 0)
    for load in loads[2:]:
        load.start()

    def cross(src, dst):
        pltpu.make_async_remote_copy(
            src_ref=src, dst_ref=dst, send_sem=cross_send, recv_sem=cross_recv,
            device_id={"ctx": partner}, device_id_type=MESH,
        ).start()

    def in_plane(n, moves):
        def one(k, carry):
            place, peer = plane_device(k)
            for slot, src, dst in moves(place, peer):
                pltpu.make_async_remote_copy(
                    src_ref=src, dst_ref=dst, send_sem=plane_send.at[n], recv_sem=plane_recv.at[slot],
                    device_id={"ctx": peer}, device_id_type=MESH,
                ).start()
            return carry

        lax.fori_loop(1, half, one, 0)

    def wait_rows(ref, n_rows, sem):
        part = ref.at[pl.ds(0, n_rows)]
        pltpu.make_async_copy(part, part, sem).wait()

    def send_own(n):
        in_plane(n, lambda place, peer: [(n, sent.at[n, block(z * half + place)], arrived.at[n, block(me)])])
        arrived[n, block(me)] = sent[n, block(z * half + i)]

    def send_on(n):
        wait_rows(crossed, side, cross_recv)
        in_plane(n, lambda place, peer: [(n, crossed.at[block(place)], arrived.at[n, block(partner)])])
        arrived[n, block(partner)] = crossed[block(i)]

    def to_all(n, recv, source, dst):
        def one(k, carry):
            peer = lax.rem(me + k, blocks)
            pltpu.make_async_remote_copy(
                src_ref=source(peer), dst_ref=dst, send_sem=plane_send.at[n], recv_sem=plane_recv.at[recv],
                device_id={"ctx": peer}, device_id_type=MESH,
            ).start()
            return carry

        lax.fori_loop(1, blocks, one, 0)

    def owner_block(device):
        return block(lax.rem(lax.div(device, 2), 2) * half + 2 * lax.div(device, 4) + lax.rem(device, 2))

    def send_direct(n):
        to_all(n, n, lambda peer: sent.at[n, owner_block(peer)], arrived.at[n, block(me)])
        arrived[n, block(me)] = sent[n, owner_block(me)]

    def give(n, target):
        to_all(n, n, lambda peer: sent.at[n, block(peer)], target.at[owner_block(me)])

    loads[0].wait()
    loads[1].wait()
    sent[0] = (k_in[...].astype(F32) * v_in[...].astype(F32)).astype(BF16)
    pl.semaphore_wait(barrier, half)
    cross(sent.at[0, part_of(1 - z)], crossed)
    pl.semaphore_signal(ready, inc=1, device_id={"ctx": partner}, device_id_type=MESH)
    loads[2].wait()
    sent[1] = taps_in[...].astype(BF16)
    loads[3].wait()
    loads[4].wait()
    sent[2] = (g_in[...].astype(F32) * q_in[...].astype(F32)).astype(BF16)
    pl.semaphore_wait(ready, 1)
    send_direct(1)
    send_own(0)
    send_direct(2)
    for load in loads[5:]:
        load.wait()

    group = 4
    tile = group * blocks

    def transform(n, spec):
        wait_rows(arrived.at[n], rows - (2 if n == 0 else 1) * count, plane_recv.at[n])
        for h in range(halves):
            wide[h] = arrived[n, :, lanes * h : lanes * (h + 1)].astype(F32)

        for t in range(count // group):
            held = packed.at[t]
            for s in range(group):
                every = pl.ds(t * group + s, blocks, stride=count)
                x = jnp.concatenate([wide[h, every, :] for h in range(halves)], axis=1).astype(BF16)
                y = dot(first[...], jnp.concatenate([x, x], axis=0))
                real, imag = y[:blocks], y[blocks:]
                cos, sin = twist[:blocks], twist[blocks:]
                part = slice(s * blocks, (s + 1) * blocks)
                held[0, part, :width], held[1, part, :width] = split(real * cos + imag * sin)
                held[0, part, width:], held[1, part, width:] = split(imag * cos - real * sin)
            spec[t * tile : (t + 1) * tile, :] = dot_split(held, forth)

    def multiply_back(n, left, right, conjugate, scale):
        for t in range(count // group):
            held = mixed.at[t]
            part = slice(t * tile, (t + 1) * tile)
            lr, li = left[part, :width], left[part, width:]
            rr, ri = right[part, :width], right[part, width:]
            if conjugate:
                held[0, :, :width], held[1, :, :width] = split(lr * rr + li * ri)
                held[0, :, width:], held[1, :, width:] = split(li * rr - lr * ri)
            else:
                held[0, :, :width], held[1, :, :width] = split(lr * rr - li * ri)
                held[0, :, width:], held[1, :, width:] = split(lr * ri + li * rr)
            u = dot_split(held, back)
            cos, sin = twist[:blocks] * scale, twist[blocks:] * scale
            for s in range(group):
                real = u[s * blocks : (s + 1) * blocks, :width]
                imag = u[s * blocks : (s + 1) * blocks, width:]
                high, low = split(jnp.concatenate([real * cos - imag * sin, imag * cos + real * sin], axis=0))
                out = dot(last[...], jnp.concatenate([high, high, low], axis=0))
                for h in range(halves):
                    wide[h, pl.ds(t * group + s, blocks, stride=count), :] = out[:, lanes * h : lanes * (h + 1)]
        for h in range(halves):
            sent[n, :, lanes * h : lanes * (h + 1)] = wide[h].astype(BF16)

    norm = 1.0 / (blocks * width)
    fwd, bwd = returned.at[0], returned.at[1]
    send_on(0)
    transform(0, gated_spec)
    transform(1, taps_spec)
    multiply_back(3, gated_spec, taps_spec, False, norm)
    give(3, fwd)
    fwd[owner_block(me)] = sent[3, block(me)]
    transform(2, prod_spec)
    multiply_back(4, prod_spec, taps_spec, True, norm)
    give(4, bwd)
    bwd[owner_block(me)] = sent[4, block(me)]
    multiply_back(5, prod_spec, gated_spec, True, norm * (blocks * width) ** -0.5)
    give(5, tap_out)
    own_taps = pltpu.make_async_copy(sent.at[5, block(me)], tap_out.at[owner_block(me)], own_sem)
    own_taps.start()

    skip_cols = skip_in[...].T

    def each_part(body):
        for s in range(rows // lanes):
            body(pl.ds(s * lanes, lanes), skip_cols[:, s : s + 1])

    def finish_q(part, skip):
        total = returned[0, part].astype(F32) + skip * sent[0, part].astype(F32)
        q_out[part] = (g_in[part].astype(F32) * total).astype(BF16)

    def finish_kv(part, skip):
        z_grad = returned[1, part].astype(F32) + skip * sent[2, part].astype(F32)
        k_out[part] = (v_in[part].astype(F32) * z_grad).astype(BF16)
        v_out[part] = (k_in[part].astype(F32) * z_grad).astype(BF16)

    stores = [
        pltpu.make_async_copy(src, dst, store_sem.at[n])
        for n, (src, dst) in enumerate(((q_out, q_hbm_out), (k_out, k_hbm_out), (v_out, v_hbm_out)))
    ]
    wait_rows(fwd, rows - count, plane_recv.at[3])
    each_part(finish_q)
    stores[0].start()
    wait_rows(bwd, rows - count, plane_recv.at[4])
    each_part(finish_kv)
    stores[1].start()
    stores[2].start()
    own_taps.wait()
    for store in stores:
        store.wait()
    wait_rows(crossed, side, cross_send)
    for n in range(6):
        wait_rows(sent.at[n], rows - (2 if n == 0 else 1) * count, plane_send.at[n])
    wait_rows(tap_out, rows - count, plane_recv.at[5])


def store_kernel(q_ref, k_ref, v_ref, tap_ref, q_out, k_out, v_out, tap_out, held, wide, sems):
    parts = 2
    step = wide.shape[0] // parts
    moves = []
    for i, (src, dst) in enumerate(((tap_ref, tap_out), (q_ref, q_out), (k_ref, k_out), (v_ref, v_out))):
        for p in range(parts):
            rows = pl.ds(p * step, step)
            stage = wide.at[rows] if i == 0 else held.at[i, rows]
            load = pltpu.make_async_copy(src.at[rows], held.at[i, rows], sems.at[0, i, p])
            store = pltpu.make_async_copy(stage, dst.at[rows], sems.at[1, i, p])
            load.start()
            moves.append((load, store, i, rows))
    for load, store, i, rows in moves:
        load.wait()
        if i == 0:
            wide[rows] = held[0, rows].astype(F32)
        store.start()
    for _, store, _, _ in moves:
        store.wait()


def exchange_convolve(k_field, v_field, out_grad, q_field, taps, skip, blocks):
    channels, width = k_field.shape
    count = channels // blocks
    rows = channels
    lanes = 128
    tables = make_tables(blocks, width)
    hbm = pl.BlockSpec(memory_space=pltpu.HBM)
    field = pltpu.VMEM((rows, width), BF16)
    spectrum = pltpu.VMEM((rows, 2 * width), F32)
    table_space = [pltpu.VMEM(t.shape, t.dtype) for t in tables]
    dma = pltpu.SemaphoreType.DMA
    result = jax.ShapeDtypeStruct((rows, width), BF16)
    grads = pl.pallas_call(
        functools.partial(kernel, blocks, count, width),
        out_shape=[result] * 4,
        in_specs=[hbm] * 11,
        out_specs=[hbm] * 4,
        scratch_shapes=[
            field, field, field, field, field, field, field,
            pltpu.VMEM((rows, width), F32), pltpu.VMEM((rows // lanes, lanes), F32), *table_space,
            pltpu.VMEM((6, rows, width), BF16),
            pltpu.VMEM((rows // 2, width), BF16),
            pltpu.VMEM((3, rows, width), BF16),
            pltpu.VMEM((2, rows, width), BF16),
            pltpu.VMEM((count // 4, 2, 4 * blocks, 2 * width), BF16),
            pltpu.VMEM((width // lanes, rows, lanes), F32),
            spectrum, spectrum, spectrum,
            pltpu.VMEM((count // 4, 2, 4 * blocks, 2 * width), BF16),
            dma((11,)), dma((3,)), dma, pltpu.SemaphoreType.REGULAR, dma, dma, dma((6,)), dma((6,)),
        ],
        compiler_params=pltpu.CompilerParams(
            collective_id=0, has_side_effects=True, vmem_limit_bytes=58 * 2**20
        ),
        name="exchange_convolve",
    )(
        k_field, v_field, out_grad, q_field, taps, skip.reshape(rows // lanes, lanes),
        *[jnp.asarray(t) for t in tables],
    )
    return pl.pallas_call(
        store_kernel,
        out_shape=[result] * 3 + [jax.ShapeDtypeStruct((rows, width), F32)],
        in_specs=[hbm] * 4,
        out_specs=[hbm] * 4,
        scratch_shapes=[pltpu.VMEM((4, rows, width), BF16), pltpu.VMEM((rows, width), F32), dma((2, 4, 2))],
        compiler_params=pltpu.CompilerParams(vmem_limit_bytes=58 * 2**20),
        name="store_grads",
    )(*grads)


def local(blocks, q_field, k_field, v_field, out_grad, filter_taps, skip):
    return tuple(exchange_convolve(k_field, v_field, out_grad, q_field, filter_taps, skip, blocks))


def solution(mesh):
    spec = P("tp", "ctx")
    return jax.shard_map(
        functools.partial(local, mesh.shape["ctx"]),
        mesh=mesh,
        in_specs=(spec, spec, spec, spec, spec, P("tp")),
        out_specs=(spec, spec, spec, spec),
        check_vma=False,
    )
```

```python
import functools

import jax
import jax.numpy as jnp
import ml_dtypes
import numpy as np
from jax import lax
from jax.experimental import pallas as pl
from jax.experimental.pallas import tpu as pltpu
from jax.sharding import PartitionSpec as P

MESH = pl.DeviceIdType.MESH
BF16 = jnp.bfloat16
F32 = jnp.float32


def split_table(table):
    high = table.astype(ml_dtypes.bfloat16)
    return high, (table - high.astype(np.float64)).astype(ml_dtypes.bfloat16)


def split(x):
    high = x.astype(BF16)
    return high, (x - high.astype(F32)).astype(BF16)


def make_tables(blocks, width):
    a = np.arange(blocks)[:, None]
    c = np.arange(blocks)[None, :] + 0.5
    phase = 2 * np.pi * a * c / (2 * blocks)
    first = np.concatenate(split_table(np.concatenate([np.cos(phase).T, -np.sin(phase).T], axis=0)), axis=1)
    high, low = split_table(np.concatenate([np.cos(phase), -np.sin(phase)], axis=1))
    last = np.concatenate([high, low, high], axis=1)
    b = np.arange(width)
    turn = 2 * np.pi * c.T * b[None, :] / (2 * blocks * width)
    twist = np.concatenate([np.cos(turn), np.sin(turn)], axis=0).astype(np.float32)
    angle = 2 * np.pi * ((b[:, None] * b[None, :]) % width) / width
    cos, sin = np.cos(angle), np.sin(angle)
    forth = np.stack(split_table(np.block([[cos, -sin], [sin, cos]])))
    back = np.stack(split_table(np.block([[cos, sin], [-sin, cos]])))
    return first, last, twist, forth, back


def dot(x, y):
    return jnp.dot(x, y, preferred_element_type=F32)


def dot_split(x, table):
    return dot(
        jnp.concatenate([x[0], x[0], x[1]], axis=1), jnp.concatenate([table[0], table[1], table[0]], axis=0)
    )


def kernel(
    blocks, count, width,
    k_hbm, v_hbm, g_hbm, q_hbm, taps_hbm, skip_hbm, first_hbm, last_hbm, twist_hbm, forth_hbm, back_hbm,
    q_hbm_out, k_hbm_out, v_hbm_out, tap_out,
    q_out, k_out, v_out, k_in, v_in, g_in, q_in, taps_in, skip_in, first, last, twist, forth, back,
    sent, crossed, arrived, returned, packed, wide, gated_spec, taps_spec, prod_spec, mixed,
    load_sem, store_sem, own_sem, ready, cross_send, cross_recv, plane_send, plane_recv,
):
    me = lax.axis_index("ctx")
    half = blocks // 2
    z = lax.rem(lax.div(me, 2), 2)
    i = 2 * lax.div(me, 4) + lax.rem(me, 2)
    partner = me + 2 - 4 * z
    rows = blocks * count
    side = half * count
    lanes = 128
    halves = width // lanes
    loads = [
        pltpu.make_async_copy(src, dst, load_sem.at[n])
        for n, (src, dst) in enumerate(
            (
                (k_hbm, k_in), (v_hbm, v_in), (taps_hbm, taps_in), (g_hbm, g_in), (q_hbm, q_in),
                (skip_hbm, skip_in), (first_hbm, first), (last_hbm, last), (twist_hbm, twist), (forth_hbm, forth), (back_hbm, back),
            )
        )
    ]
    for load in loads[:2]:
        load.start()

    def block(index):
        return pl.ds(pl.multiple_of(index * count, count), count)

    def part_of(which):
        return pl.ds(pl.multiple_of(which * side, side), side)

    def plane_device(k):
        place = lax.rem(i + k, half)
        return place, 4 * lax.div(place, 2) + 2 * z + lax.rem(place, 2)

    barrier = pltpu.get_barrier_semaphore()
    pl.semaphore_signal(barrier, inc=1, device_id={"ctx": partner}, device_id_type=MESH)

    def greet(k, carry):
        _, peer = plane_device(k)
        pl.semaphore_signal(barrier, inc=1, device_id={"ctx": peer}, device_id_type=MESH)
        return carry

    lax.fori_loop(1, half, greet, 0)
    for load in loads[2:]:
        load.start()

    def cross(src, dst):
        pltpu.make_async_remote_copy(
            src_ref=src, dst_ref=dst, send_sem=cross_send, recv_sem=cross_recv,
            device_id={"ctx": partner}, device_id_type=MESH,
        ).start()

    def in_plane(n, moves):
        def one(k, carry):
            place, peer = plane_device(k)
            for slot, src, dst in moves(place, peer):
                pltpu.make_async_remote_copy(
                    src_ref=src, dst_ref=dst, send_sem=plane_send.at[n], recv_sem=plane_recv.at[slot],
                    device_id={"ctx": peer}, device_id_type=MESH,
                ).start()
            return carry

        lax.fori_loop(1, half, one, 0)

    def wait_rows(ref, n_rows, sem):
        part = ref.at[pl.ds(0, n_rows)]
        pltpu.make_async_copy(part, part, sem).wait()

    def send_own(n):
        in_plane(n, lambda place, peer: [(n, sent.at[n, block(z * half + place)], arrived.at[n, block(me)])])
        arrived[n, block(me)] = sent[n, block(z * half + i)]

    def send_on(n):
        wait_rows(crossed, side, cross_recv)
        in_plane(n, lambda place, peer: [(n, crossed.at[block(place)], arrived.at[n, block(partner)])])
        arrived[n, block(partner)] = crossed[block(i)]

    def to_all(n, recv, source, dst):
        def one(k, carry):
            peer = lax.rem(me + k, blocks)
            pltpu.make_async_remote_copy(
                src_ref=source(peer), dst_ref=dst, send_sem=plane_send.at[n], recv_sem=plane_recv.at[recv],
                device_id={"ctx": peer}, device_id_type=MESH,
            ).start()
            return carry

        lax.fori_loop(1, blocks, one, 0)

    def owner_block(device):
        return block(lax.rem(lax.div(device, 2), 2) * half + 2 * lax.div(device, 4) + lax.rem(device, 2))

    def send_direct(n):
        to_all(n, n, lambda peer: sent.at[n, owner_block(peer)], arrived.at[n, block(me)])
        arrived[n, block(me)] = sent[n, owner_block(me)]

    def give(n, target):
        to_all(n, n, lambda peer: sent.at[n, block(peer)], target.at[owner_block(me)])

    loads[0].wait()
    loads[1].wait()
    sent[0] = (k_in[...].astype(F32) * v_in[...].astype(F32)).astype(BF16)
    pl.semaphore_wait(barrier, half)
    pl.semaphore_signal(ready, inc=1, device_id={"ctx": partner}, device_id_type=MESH)
    cross(sent.at[0, part_of(1 - z)], crossed)
    loads[2].wait()
    sent[1] = taps_in[...].astype(BF16)
    loads[3].wait()
    loads[4].wait()
    sent[2] = (g_in[...].astype(F32) * q_in[...].astype(F32)).astype(BF16)
    pl.semaphore_wait(ready, 1)
    send_direct(1)
    send_own(0)
    send_direct(2)
    for load in loads[5:]:
        load.wait()

    group = 4
    tile = group * blocks

    def transform(n, spec):
        wait_rows(arrived.at[n], rows - (2 if n == 0 else 1) * count, plane_recv.at[n])
        for h in range(halves):
            wide[h] = arrived[n, :, lanes * h : lanes * (h + 1)].astype(F32)

        for t in range(count // group):
            held = packed.at[t]
            for s in range(group):
                every = pl.ds(t * group + s, blocks, stride=count)
                x = jnp.concatenate([wide[h, every, :] for h in range(halves)], axis=1).astype(BF16)
                y = dot(first[...], jnp.concatenate([x, x], axis=0))
                real, imag = y[:blocks], y[blocks:]
                cos, sin = twist[:blocks], twist[blocks:]
                part = slice(s * blocks, (s + 1) * blocks)
                held[0, part, :width], held[1, part, :width] = split(real * cos + imag * sin)
                held[0, part, width:], held[1, part, width:] = split(imag * cos - real * sin)
            spec[t * tile : (t + 1) * tile, :] = dot_split(held, forth)

    def multiply_back(n, left, right, conjugate, scale):
        for t in range(count // group):
            held = mixed.at[t]
            part = slice(t * tile, (t + 1) * tile)
            lr, li = left[part, :width], left[part, width:]
            rr, ri = right[part, :width], right[part, width:]
            if conjugate:
                held[0, :, :width], held[1, :, :width] = split(lr * rr + li * ri)
                held[0, :, width:], held[1, :, width:] = split(li * rr - lr * ri)
            else:
                held[0, :, :width], held[1, :, :width] = split(lr * rr - li * ri)
                held[0, :, width:], held[1, :, width:] = split(lr * ri + li * rr)
            u = dot_split(held, back)
            cos, sin = twist[:blocks] * scale, twist[blocks:] * scale
            for s in range(group):
                real = u[s * blocks : (s + 1) * blocks, :width]
                imag = u[s * blocks : (s + 1) * blocks, width:]
                high, low = split(jnp.concatenate([real * cos - imag * sin, imag * cos + real * sin], axis=0))
                out = dot(last[...], jnp.concatenate([high, high, low], axis=0))
                for h in range(halves):
                    wide[h, pl.ds(t * group + s, blocks, stride=count), :] = out[:, lanes * h : lanes * (h + 1)]
        for h in range(halves):
            sent[n, :, lanes * h : lanes * (h + 1)] = wide[h].astype(BF16)

    norm = 1.0 / (blocks * width)
    fwd, bwd = returned.at[0], returned.at[1]
    send_on(0)
    transform(0, gated_spec)
    transform(1, taps_spec)
    multiply_back(3, gated_spec, taps_spec, False, norm)
    give(3, fwd)
    fwd[owner_block(me)] = sent[3, block(me)]
    transform(2, prod_spec)
    multiply_back(4, prod_spec, taps_spec, True, norm)
    give(4, bwd)
    bwd[owner_block(me)] = sent[4, block(me)]
    multiply_back(5, prod_spec, gated_spec, True, norm * (blocks * width) ** -0.5)
    give(5, tap_out)
    own_taps = pltpu.make_async_copy(sent.at[5, block(me)], tap_out.at[owner_block(me)], own_sem)
    own_taps.start()

    skip_cols = skip_in[...].T

    def each_part(body):
        for s in range(rows // lanes):
            body(pl.ds(s * lanes, lanes), skip_cols[:, s : s + 1])

    def finish_q(part, skip):
        total = returned[0, part].astype(F32) + skip * sent[0, part].astype(F32)
        q_out[part] = (g_in[part].astype(F32) * total).astype(BF16)

    def finish_kv(part, skip):
        z_grad = returned[1, part].astype(F32) + skip * sent[2, part].astype(F32)
        k_out[part] = (v_in[part].astype(F32) * z_grad).astype(BF16)
        v_out[part] = (k_in[part].astype(F32) * z_grad).astype(BF16)

    stores = [
        pltpu.make_async_copy(src, dst, store_sem.at[n])
        for n, (src, dst) in enumerate(((q_out, q_hbm_out), (k_out, k_hbm_out), (v_out, v_hbm_out)))
    ]
    wait_rows(fwd, rows - count, plane_recv.at[3])
    each_part(finish_q)
    stores[0].start()
    wait_rows(bwd, rows - count, plane_recv.at[4])
    each_part(finish_kv)
    stores[1].start()
    stores[2].start()
    own_taps.wait()
    for store in stores:
        store.wait()
    wait_rows(crossed, side, cross_send)
    for n in range(6):
        wait_rows(sent.at[n], rows - (2 if n == 0 else 1) * count, plane_send.at[n])
    wait_rows(tap_out, rows - count, plane_recv.at[5])


def store_kernel(q_ref, k_ref, v_ref, tap_ref, q_out, k_out, v_out, tap_out, held, wide, sems):
    parts = 2
    step = wide.shape[0] // parts
    moves = []
    for i, (src, dst) in enumerate(((tap_ref, tap_out), (q_ref, q_out), (k_ref, k_out), (v_ref, v_out))):
        for p in range(parts):
            rows = pl.ds(p * step, step)
            stage = wide.at[rows] if i == 0 else held.at[i, rows]
            load = pltpu.make_async_copy(src.at[rows], held.at[i, rows], sems.at[0, i, p])
            store = pltpu.make_async_copy(stage, dst.at[rows], sems.at[1, i, p])
            load.start()
            moves.append((load, store, i, rows))
    for load, store, i, rows in moves:
        load.wait()
        if i == 0:
            wide[rows] = held[0, rows].astype(F32)
        store.start()
    for _, store, _, _ in moves:
        store.wait()


def exchange_convolve(k_field, v_field, out_grad, q_field, taps, skip, blocks):
    channels, width = k_field.shape
    count = channels // blocks
    rows = channels
    lanes = 128
    tables = make_tables(blocks, width)
    hbm = pl.BlockSpec(memory_space=pltpu.HBM)
    field = pltpu.VMEM((rows, width), BF16)
    spectrum = pltpu.VMEM((rows, 2 * width), F32)
    table_space = [pltpu.VMEM(t.shape, t.dtype) for t in tables]
    dma = pltpu.SemaphoreType.DMA
    result = jax.ShapeDtypeStruct((rows, width), BF16)
    grads = pl.pallas_call(
        functools.partial(kernel, blocks, count, width),
        out_shape=[result] * 4,
        in_specs=[hbm] * 11,
        out_specs=[hbm] * 4,
        scratch_shapes=[
            field, field, field, field, field, field, field,
            pltpu.VMEM((rows, width), F32), pltpu.VMEM((rows // lanes, lanes), F32), *table_space,
            pltpu.VMEM((6, rows, width), BF16),
            pltpu.VMEM((rows // 2, width), BF16),
            pltpu.VMEM((3, rows, width), BF16),
            pltpu.VMEM((2, rows, width), BF16),
            pltpu.VMEM((count // 4, 2, 4 * blocks, 2 * width), BF16),
            pltpu.VMEM((width // lanes, rows, lanes), F32),
            spectrum, spectrum, spectrum,
            pltpu.VMEM((count // 4, 2, 4 * blocks, 2 * width), BF16),
            dma((11,)), dma((3,)), dma, pltpu.SemaphoreType.REGULAR, dma, dma, dma((6,)), dma((6,)),
        ],
        compiler_params=pltpu.CompilerParams(
            collective_id=0, has_side_effects=True, vmem_limit_bytes=58 * 2**20
        ),
        name="exchange_convolve",
    )(
        k_field, v_field, out_grad, q_field, taps, skip.reshape(rows // lanes, lanes),
        *[jnp.asarray(t) for t in tables],
    )
    return pl.pallas_call(
        store_kernel,
        out_shape=[result] * 3 + [jax.ShapeDtypeStruct((rows, width), F32)],
        in_specs=[hbm] * 4,
        out_specs=[hbm] * 4,
        scratch_shapes=[pltpu.VMEM((4, rows, width), BF16), pltpu.VMEM((rows, width), F32), dma((2, 4, 2))],
        compiler_params=pltpu.CompilerParams(vmem_limit_bytes=58 * 2**20),
        name="store_grads",
    )(*grads)


def local(blocks, q_field, k_field, v_field, out_grad, filter_taps, skip):
    return tuple(exchange_convolve(k_field, v_field, out_grad, q_field, filter_taps, skip, blocks))


def solution(mesh):
    spec = P("tp", "ctx")
    return jax.shard_map(
        functools.partial(local, mesh.shape["ctx"]),
        mesh=mesh,
        in_specs=(spec, spec, spec, spec, spec, P("tp")),
        out_specs=(spec, spec, spec, spec),
        check_vma=False,
    )
```
